256 devices in a mesh: rows: 64 (over y, z, core), pairs: 4 (over x).
Axes of the slice: x: 4, y: 4, z: 8, core: 2. Of those that a mesh axis runs over, the one named last changes fastest.
Arguments:
- factor_rows: bfloat16 [32768, 256], P('rows'), may hold values from -6 to 6
- row_side_probes: bfloat16 [32768, 128], P('rows'), may hold values from -6 to 6
- factor_cols: bfloat16 [32768, 256], P(('rows', 'pairs')), may hold values from -0.375 to 0.375
- probe_cols: bfloat16 [32768, 128], P(('rows', 'pairs')), may hold values from -6 to 6
- pair_blocks: int32 [64, 64], P('rows'), may hold values from 0 to 63, as said below
- pair_count: int32 [64], P('rows'), may hold values from 32 to 64, as said below
Outputs:
- row_sketch: float32 [32768, 128], P(('rows', 'pairs'))
- col_sketch: float32 [32768, 128], P(('rows', 'pairs'))
- sketch_gram: float32 [128, 128], replicated
The draws below stay inside these ranges and needn't reach their ends.
Inputs may be any that keep to these rules, and one draw needn't show every extreme that they name: `pair_blocks`: the entries of one row are distinct. `pair_count`: some row block has exactly 64 pairs.
All inputs are finite; a program needn't handle non-finite values.
Results may differ from the reference program's by a relative error of at most 0.003.
Values may be sent and summed in bfloat16 or wider, within the bound.
No kernel may reach another device: no remote copies, remote signals or barrier semaphores. Data moves between devices by JAX's collectives and lax.ppermute only.
A program may use at most 64 MiB of HBM per device.

```python
import math
import jax
import jax.numpy as jnp
from jax import lax

RANK = 256
PROBES = 128
ROWS_DEV = 512
NODES = 32768
SLOTS = 64
N_ROWS = 64


def draw_pair_blocks(key, part):
    key = jax.random.fold_in(key, 11)
    row_keys = jax.random.split(key, N_ROWS)
    chosen = jax.vmap(lambda row_key: jax.random.permutation(row_key, N_ROWS)[:SLOTS])(row_keys)
    return chosen.astype(jnp.int32)


def draw_pair_count(key, part):
    key = jax.random.fold_in(key, 12)
    base_key, heavy_key, forced_key = jax.random.split(key, 3)
    lowest = N_ROWS // 2
    base = jax.random.randint(base_key, (N_ROWS,), lowest, 3 * N_ROWS // 4 + 1)
    heavy = jax.random.randint(heavy_key, (N_ROWS,), 0, 8) == 0
    counts = jnp.where(heavy, SLOTS, base)
    forced = jax.random.randint(forced_key, (), 0, N_ROWS)
    counts = counts.at[forced].set(SLOTS)
    counts = counts.at[(forced + 1) % N_ROWS].set(lowest)
    return counts.astype(jnp.int32)


def level_of(key, shape, cuts, low, top_value):
    gain = 1.0
    for axis_at, shards_of in cuts:
        steps = jax.random.uniform(jax.random.fold_in(jax.random.fold_in(key, 6), axis_at), (shards_of,), jnp.float32, low / len(cuts), top_value / len(cuts))
        gain = gain * jnp.repeat(jnp.exp(steps), shape[axis_at] // shards_of).reshape((-1,) + (1,) * (len(shape) - 1 - axis_at))
    return gain


def gaussian(own_key, extent, width, reach, pieces=(), held_as=jnp.bfloat16):
    drawn = width * jax.random.normal(own_key, extent, jnp.float32)
    if pieces:
        drawn = drawn * level_of(own_key, extent, pieces, -0.22, 0.18)
    return jnp.clip(drawn, -reach, reach).astype(held_as)


def setup_inputs(seed: int = 0) -> dict:
    key_of = jax.random.split(jax.random.key(seed), 7)
    return {
        "factor_rows": gaussian(key_of[0], (NODES, RANK), 1.0, 6.0, ((0, 64),)),
        "row_side_probes": gaussian(key_of[1], (NODES, PROBES), 1.0, 6.0, ((0, 64),)),
        "factor_cols": gaussian(key_of[2], (NODES, RANK), RANK ** -0.5, 0.375, ((0, 256),)),
        "probe_cols": gaussian(key_of[3], (NODES, PROBES), 1.0, 6.0, ((0, 256),)),
        "pair_blocks": draw_pair_blocks(jax.random.fold_in(key_of[6], 71), 0),
        "pair_count": draw_pair_count(jax.random.fold_in(key_of[6], 71), 0),
    }


def reference(factor_rows, row_side_probes, factor_cols, probe_cols, pair_blocks, pair_count):
    sketch_scale = 1.0 / math.sqrt(SLOTS * ROWS_DEV)
    row_total = jnp.zeros((NODES, PROBES), jnp.float32)
    col_total = jnp.zeros((NODES, PROBES), jnp.float32)

    def one_block(block_index, carry):
        row_accumulator, col_acc = carry
        start = (block_index * ROWS_DEV).astype(jnp.int32)
        left = lax.dynamic_slice_in_dim(factor_rows, start, ROWS_DEV, 0)
        source_gaussian_draws = lax.dynamic_slice_in_dim(row_side_probes, start, ROWS_DEV, 0)

        def one_pair(slot_index, inner):
            horizontal_share, col_part = inner
            target = pair_blocks[block_index, slot_index]
            col_start = (target * ROWS_DEV).astype(jnp.int32)
            right = lax.dynamic_slice_in_dim(factor_cols, col_start, ROWS_DEV, 0)
            target_gaussian_draws = lax.dynamic_slice_in_dim(probe_cols, col_start, ROWS_DEV, 0)
            kernel_weights = jnp.dot(left, right.T, preferred_element_type=jnp.float32)
            nearness_kernel = jnp.log(jnp.maximum(4.0 * kernel_weights, 1.0)).astype(jnp.bfloat16)
            horizontal_share = horizontal_share + jnp.dot(nearness_kernel, target_gaussian_draws, preferred_element_type=jnp.float32)
            vertical_sketch_entries = jnp.dot(nearness_kernel.T, source_gaussian_draws, preferred_element_type=jnp.float32)
            previous = lax.dynamic_slice_in_dim(col_part, col_start, ROWS_DEV, 0)
            col_part = lax.dynamic_update_slice_in_dim(col_part, previous + vertical_sketch_entries, col_start, 0)
            return (horizontal_share, col_part)
        row_zero = jnp.zeros((ROWS_DEV, PROBES), jnp.float32)
        horizontal_share, col_acc = lax.fori_loop(0, pair_count[block_index], one_pair, (row_zero, col_acc))
        row_accumulator = lax.dynamic_update_slice_in_dim(row_accumulator, horizontal_share, start, 0)
        return (row_accumulator, col_acc)
    row_total, col_total = lax.fori_loop(0, N_ROWS, one_block, (row_total, col_total))
    row_sketch = row_total * sketch_scale
    col_sketch = col_total * sketch_scale
    sketch_gram = jnp.dot(row_side_probes.astype(jnp.float32).T, row_sketch, precision=lax.Precision.HIGHEST) / math.sqrt(NODES)
    return (row_sketch, col_sketch, sketch_gram)
```

```python
import math

import jax
import jax.numpy as jnp
from jax import lax
from jax.experimental import pallas as pl
from jax.experimental.pallas import tpu as pltpu
from jax.sharding import Mesh, PartitionSpec as P

BF16 = jnp.bfloat16
F32 = jnp.float32
Y, Z, C, X = 4, 8, 2, 4
BLOCK, SUB, RANK, PROBES = 512, 128, 256, 128
WIDTH = RANK + PROBES
MASK_ROWS = 16
HALF = Z * SUB
NODES = Y * Z * C * BLOCK


def tile_kernel(scale_ref, rows_ref, own_ref, other_ref, row_ref, keep_ref, send_ref, row_acc, col_acc):
    def step(turn, _):
        block = turn // 2
        half = turn - 2 * block

        def run(cols_ref):
            left = rows_ref[block, 0:BLOCK, 0:RANK]
            left_probes = rows_ref[block, 0:BLOCK, RANK:WIDTH]
            right = jnp.concatenate(
                [cols_ref[s, :, 0:RANK] * scale_ref[block, half * Z + s].astype(BF16) for s in range(Z)], 0
            )
            right_probes = cols_ref[:, :, RANK:WIDTH].reshape(HALF, PROBES)
            scores = lax.dot_general(left, right, (((1,), (1,)), ((), ())), preferred_element_type=F32)
            proximity = jnp.log(jnp.maximum(scores, 1.0)).astype(BF16)
            row_part = jnp.dot(proximity, right_probes, preferred_element_type=F32)
            col_part = lax.dot_general(left_probes, proximity, (((0,), (0,)), ((), ())), preferred_element_type=F32)

            @pl.when(half == 0)
            def _():
                row_acc[block] = row_part

            @pl.when(half == 1)
            def _():
                row_acc[block] += row_part

            @pl.when(block == 0)
            def _():
                col_acc[half] = col_part

            @pl.when(block > 0)
            def _():
                col_acc[half] += col_part

        @pl.when(half == 0)
        def _():
            run(own_ref)

        @pl.when(half == 1)
        def _():
            run(other_ref)

        return 0

    lax.fori_loop(0, 2 * Y, step, 0)
    gram = jnp.zeros((PROBES, PROBES), F32)
    for block in range(Y):
        total = row_acc[block]
        high = total.astype(BF16)
        low = (total - high.astype(F32)).astype(BF16)
        row_ref[block] = high
        left_probes = rows_ref[block, 0:BLOCK, RANK:WIDTH]
        for part in (high, low):
            gram += lax.dot_general(left_probes, part, (((0,), (0,)), ((), ())), preferred_element_type=F32)
    for s in range(Z):
        keep_ref[s] = col_acc[0, :, s * SUB : (s + 1) * SUB]
        send_ref[s] = col_acc[1, :, s * SUB : (s + 1) * SUB]
    keep_ref[Z] = gram
    send_ref[Z] = gram


def split(value):
    high = value.astype(BF16)
    low = (value - high.astype(F32)).astype(BF16)
    return high, low


def shards(factor_rows, row_side_probes, factor_cols, probe_cols, pair_blocks, pair_count):
    scale = 1.0 / math.sqrt(NODES)
    y, c = lax.axis_index("y"), lax.axis_index("c")
    live = lax.iota(jnp.int32, Y * Z * C)[:, None] < pair_count[0]
    hits = (pair_blocks[0][:, None] == lax.iota(jnp.int32, Y * Z * C)[None, :]) & live
    used = jnp.any(hits, axis=0).astype(BF16)
    used_rows = jnp.pad(used[None, :], ((0, MASK_ROWS - 1), (0, WIDTH - Y * Z * C)))
    row_load = jnp.concatenate([jnp.concatenate([factor_rows, row_side_probes], 1), used_rows], 0)
    all_rows = lax.all_gather(row_load, "y", axis=0, tiled=False)

    col_load = jnp.concatenate([factor_cols, probe_cols], 1)
    own_cols = lax.all_to_all(
        jnp.broadcast_to(col_load[None], (Z, SUB, WIDTH)), "z", split_axis=0, concat_axis=0, tiled=True
    )
    other_cols = lax.ppermute(own_cols, "c", [(0, 1), (1, 0)])

    flags = lax.dynamic_slice_in_dim(all_rows[:, BLOCK, : Y * Z * C], y * Z * C, Z * C, 1)
    flags = 4.0 * flags.astype(F32).reshape(Y, Z, C)
    flags = jnp.stack([lax.dynamic_index_in_dim(flags, c, 2, False), lax.dynamic_index_in_dim(flags, 1 - c, 2, False)], 1)
    flags = flags.reshape(Y, C * Z)

    vmem = pl.BlockSpec(memory_space=pltpu.VMEM)
    row_part, keep, send = pl.pallas_call(
        tile_kernel,
        out_shape=[
            jax.ShapeDtypeStruct((Y, BLOCK, PROBES), BF16),
            jax.ShapeDtypeStruct((Z + 1, PROBES, SUB), F32),
            jax.ShapeDtypeStruct((Z + 1, PROBES, SUB), F32),
        ],
        in_specs=[pl.BlockSpec(memory_space=pltpu.SMEM), vmem, vmem, vmem],
        out_specs=[vmem, vmem, vmem],
        scratch_shapes=[pltpu.VMEM((Y, BLOCK, PROBES), F32), pltpu.VMEM((C, PROBES, HALF), F32)],
        compiler_params=pltpu.CompilerParams(vmem_limit_bytes=40 * 2**20),
        name="tiles",
    )(flags, all_rows, own_cols, other_cols)

    chip = keep + lax.ppermute(send, "c", [(0, 1), (1, 0)])
    gram_half = lax.dynamic_index_in_dim(chip[Z].reshape(C, X, 16, PROBES), c, 0, False)
    gram_half = jnp.broadcast_to(gram_half[None], (Y, X, 16, PROBES)).reshape(Y * X, 16, PROBES)
    row_load = jnp.concatenate([row_part.reshape(Y * X, SUB, PROBES), *split(gram_half)], 1)
    row_got = lax.all_to_all(row_load, ("y", "x"), split_axis=0, concat_axis=0, tiled=True)
    row_sum = jnp.sum(row_got.astype(F32), 0)
    row_sketch = row_sum[:SUB] * scale
    gram_piece = row_sum[SUB : SUB + 16] + row_sum[SUB + 16 :]

    gram_all_z = jnp.broadcast_to(jnp.concatenate(split(gram_piece), 0)[None], (Z, 32, PROBES))
    col_load = jnp.concatenate([chip[:Z].astype(BF16), gram_all_z], 1)
    col_got = lax.all_to_all(col_load, "z", split_axis=0, concat_axis=0, tiled=True)
    col_sum = jnp.sum(col_got.astype(F32), 0)
    col_sketch = col_sum[:SUB].T * scale
    gram_piece = (col_sum[SUB : SUB + 16] + col_sum[SUB + 16 :]) / NODES
    sketch_gram = lax.all_gather(gram_piece, ("c", "x"), axis=0, tiled=True)
    return (row_sketch, col_sketch, sketch_gram)


def solution(mesh):
    grid = Mesh(mesh.devices.reshape(Y, Z, C, X), ("y", "z", "c", "x"))
    rows, subs = ("y", "z", "c"), ("y", "z", "c", "x")
    return jax.shard_map(
        shards,
        mesh=grid,
        in_specs=(P(rows, None), P(rows, None), P(subs, None), P(subs, None), P(rows, None), P(rows)),
        out_specs=(P(subs, None), P(subs, None), P()),
        check_vma=False,
    )
```

```python
import math

import jax
import jax.numpy as jnp
from jax import lax
from jax.experimental import pallas as pl
from jax.experimental.pallas import tpu as pltpu
from jax.sharding import Mesh, PartitionSpec as P

BF16 = jnp.bfloat16
F32 = jnp.float32
Y, Z, C, X = 4, 8, 2, 4
BLOCKS = Y * Z * C
BLOCK, SUB, RANK, PROBES = 512, 128, 256, 128
WIDTH = RANK + PROBES
MASK_ROWS = 16
LOAD_ROWS = BLOCK + MASK_ROWS
HALF = Z * SUB
NODES = BLOCKS * BLOCK
PIECE = PROBES // (C * X)
SENT = SUB + 2 * PIECE
SCALE = 1.0 / math.sqrt(NODES)
LIMIT = 40 * 2**20
SWAP = [(0, 1), (1, 0)]


def contract_rows(left, right):
    return lax.dot_general(left, right, (((0,), (0,)), ((), ())), preferred_element_type=F32)


def split(value):
    high = value.astype(BF16)
    low = (value - high.astype(F32)).astype(BF16)
    return high, low


def pack_kernel(count_ref, factor_ref, side_ref, cols_ref, probe_ref, pairs_ref, rows_out, cols_out):
    slots = pairs_ref.shape[1]
    used = lax.broadcasted_iota(jnp.int32, (BLOCKS, slots), 1) < count_ref[0]
    same = lax.broadcasted_iota(jnp.int32, (BLOCKS, slots), 0) == pairs_ref[...]
    hits = jnp.where(same & used, 1.0, 0.0).astype(BF16)
    ones = jnp.ones((MASK_ROWS, slots), BF16)
    flags = lax.dot_general(ones, hits, (((1,), (1,)), ((), ())), preferred_element_type=F32)
    flags = jnp.concatenate([flags, jnp.zeros((MASK_ROWS, WIDTH - BLOCKS), F32)], 1)
    rows_out[BLOCK:LOAD_ROWS, :] = flags.astype(BF16)
    rows_out[0:BLOCK, 0:RANK] = factor_ref[...]
    rows_out[0:BLOCK, RANK:WIDTH] = side_ref[...]
    for s in range(Z):
        cols_out[s, :, 0:RANK] = cols_ref[...]
        cols_out[s, :, RANK:WIDTH] = probe_ref[...]


def tile_kernel(rows_hbm, own_ref, other_ref, row_ref, keep_ref, send_ref, rows_ref, col_acc, sems):
    copies = [pltpu.make_async_copy(rows_hbm.at[k], rows_ref.at[k], sems.at[k]) for k in range(Y)]
    for copy in copies:
        copy.start()
    first = lax.axis_index("y") * (Z * C)
    core = lax.axis_index("c")
    gram = jnp.zeros((PROBES, PROBES), F32)
    for block in range(Y):
        copies[block].wait()
        left = rows_ref[block, 0:BLOCK, 0:RANK]
        left_probes = rows_ref[block, 0:BLOCK, RANK:WIDTH]
        flags = 4.0 * rows_ref[block, BLOCK:LOAD_ROWS, 0:128].astype(F32)[0:8]
        total = None
        for half, cols_ref in enumerate((own_ref, other_ref)):
            at = first + (core if half == 0 else 1 - core)
            turned = pltpu.roll(flags, lax.rem(128 - at, 128), 1)
            right = jnp.concatenate(
                [cols_ref[s, :, 0:RANK] * turned[0:1, C * s : C * s + 1].astype(BF16) for s in range(Z)], 0
            )
            right_probes = cols_ref[:, :, RANK:WIDTH].reshape(HALF, PROBES)
            scores = lax.dot_general(left, right, (((1,), (1,)), ((), ())), preferred_element_type=F32)
            proximity = jnp.log(jnp.maximum(scores, 1.0)).astype(BF16)
            row_part = jnp.dot(proximity, right_probes, preferred_element_type=F32)
            total = row_part if half == 0 else total + row_part
            col_part = contract_rows(left_probes, proximity)
            if block == 0:
                col_acc[half] = col_part
            else:
                col_acc[half] += col_part
        high, low = split(total)
        for q in range(X):
            row_ref[X * block + q] = high[SUB * q : SUB * (q + 1)]
        gram += contract_rows(left_probes, high) + contract_rows(left_probes, low)
    for s in range(Z):
        keep_ref[s] = col_acc[0, :, s * SUB : (s + 1) * SUB]
        send_ref[s] = col_acc[1, :, s * SUB : (s + 1) * SUB]
    keep_ref[Z] = gram
    send_ref[Z] = gram


def join_kernel(keep_ref, got_ref, part_ref, rows_out, cols_out):
    for s in range(Z):
        cols_out[s, 0:SUB, :] = (keep_ref[s] + got_ref[s]).astype(BF16)
    core = lax.axis_index("c")
    half = PROBES // C
    at = pl.ds(pl.multiple_of(core * half, half), half)
    gram = keep_ref[Z, at, :] + got_ref[Z, at, :]
    high, low = split(gram)
    for y in range(Y):
        for x in range(X):
            rows_out[X * y + x, 0:SUB, :] = part_ref[X * y + x]
            rows_out[X * y + x, SUB : SUB + PIECE, :] = high[PIECE * x : PIECE * (x + 1)]
            rows_out[X * y + x, SUB + PIECE : SENT, :] = low[PIECE * x : PIECE * (x + 1)]


def row_kernel(got_ref, cols_ref, sketch_ref, cols_out):
    total = got_ref[0].astype(F32)
    for k in range(1, Y * X):
        total += got_ref[k].astype(F32)
    sketch_ref[...] = total[0:SUB] * SCALE
    high, low = split(total[SUB : SUB + PIECE] + total[SUB + PIECE : SENT])
    for s in range(Z):
        cols_out[s, 0:SUB, :] = cols_ref[s]
        cols_out[s, SUB : SUB + PIECE, :] = high
        cols_out[s, SUB + PIECE : SENT, :] = low


def col_kernel(got_ref, sketch_ref, gram_ref):
    total = got_ref[0].astype(F32)
    for k in range(1, Z):
        total += got_ref[k].astype(F32)
    sketch_ref[...] = total[0:SUB].T * SCALE
    gram_ref[...] = (total[SUB : SUB + PIECE] + total[SUB + PIECE : SENT]) * (1.0 / NODES)


def shards(factor_rows, row_side_probes, factor_cols, probe_cols, pair_blocks, pair_count):
    vmem = pl.BlockSpec(memory_space=pltpu.VMEM)
    smem = pl.BlockSpec(memory_space=pltpu.SMEM)
    hbm = pl.BlockSpec(memory_space=pl.ANY)
    params = pltpu.CompilerParams(vmem_limit_bytes=LIMIT)
    shape = jax.ShapeDtypeStruct

    row_load, col_load = pl.pallas_call(
        pack_kernel,
        out_shape=[shape((LOAD_ROWS, WIDTH), BF16), shape((Z, SUB, WIDTH), BF16)],
        in_specs=[smem, vmem, vmem, vmem, vmem, vmem],
        out_specs=[vmem, vmem],
        compiler_params=params,
        name="pack",
    )(pair_count, factor_rows, row_side_probes, factor_cols, probe_cols, pair_blocks)
    all_rows = lax.all_gather(row_load, "y", axis=0, tiled=False)
    own_cols = lax.all_to_all(col_load, "z", split_axis=0, concat_axis=0, tiled=True)
    other_cols = lax.ppermute(own_cols, "c", SWAP)

    row_part, keep, send = pl.pallas_call(
        tile_kernel,
        out_shape=[
            shape((Y * X, SUB, PROBES), BF16),
            shape((Z + 1, PROBES, SUB), F32),
            shape((Z + 1, PROBES, SUB), F32),
        ],
        in_specs=[hbm, vmem, vmem],
        out_specs=[vmem, vmem, vmem],
        scratch_shapes=[
            pltpu.VMEM((Y, LOAD_ROWS, WIDTH), BF16),
            pltpu.VMEM((C, PROBES, HALF), F32),
            pltpu.SemaphoreType.DMA((Y,)),
        ],
        compiler_params=params,
        name="tiles",
    )(all_rows, own_cols, other_cols)

    got = lax.ppermute(send, "c", SWAP)
    row_load, col_part = pl.pallas_call(
        join_kernel,
        out_shape=[shape((Y * X, SENT, PROBES), BF16), shape((Z, SUB, SUB), BF16)],
        in_specs=[vmem, vmem, vmem],
        out_specs=[vmem, vmem],
        compiler_params=params,
        name="join",
    )(keep, got, row_part)
    row_got = lax.all_to_all(row_load, ("y", "x"), split_axis=0, concat_axis=0, tiled=True)
    row_sketch, col_load = pl.pallas_call(
        row_kernel,
        out_shape=[shape((SUB, PROBES), F32), shape((Z, SENT, SUB), BF16)],
        in_specs=[vmem, vmem],
        out_specs=[vmem, vmem],
        compiler_params=params,
        name="row_sum",
    )(row_got, col_part)
    col_got = lax.all_to_all(col_load, "z", split_axis=0, concat_axis=0, tiled=True)
    col_sketch, gram = pl.pallas_call(
        col_kernel,
        out_shape=[shape((SUB, PROBES), F32), shape((PIECE, PROBES), F32)],
        in_specs=[vmem],
        out_specs=[vmem, vmem],
        compiler_params=params,
        name="col_sum",
    )(col_got)

    x, c = lax.axis_index("x"), lax.axis_index("c")
    for axis, pairs, upper in (
        ("x", [(0, 1), (1, 0), (2, 3), (3, 2)], lax.rem(x, 2) == 1),
        ("x", [(0, 3), (3, 0), (1, 2), (2, 1)], x >= 2),
        ("c", SWAP, c == 1),
    ):
        peer = lax.ppermute(gram, axis, pairs)
        gram = jnp.concatenate([jnp.where(upper, peer, gram), jnp.where(upper, gram, peer)], 0)
    return (row_sketch, col_sketch, gram)


def solution(mesh):
    grid = Mesh(mesh.devices.reshape(Y, Z, C, X), ("y", "z", "c", "x"))
    rows, subs = ("y", "z", "c"), ("y", "z", "c", "x")
    return jax.shard_map(
        shards,
        mesh=grid,
        in_specs=(P(rows, None), P(rows, None), P(subs, None), P(subs, None), P(rows, None), P(rows)),
        out_specs=(P(subs, None), P(subs, None), P()),
        check_vma=False,
    )
```

```python
import math

import jax
import jax.numpy as jnp
from jax import lax
from jax.experimental import pallas as pl
from jax.experimental.pallas import tpu as pltpu
from jax.sharding import Mesh, PartitionSpec as P

BF16 = jnp.bfloat16
F32 = jnp.float32
Y, Z, C, X = 4, 8, 2, 4
BLOCKS = Y * Z * C
BLOCK, SUB, RANK, PROBES = 512, 128, 256, 128
WIDTH = RANK + PROBES
MASK_ROWS = 16
LOAD_ROWS = BLOCK + MASK_ROWS
HALF = Z * SUB
NODES = BLOCKS * BLOCK
PIECE = PROBES // (C * X)
SENT = SUB + 2 * PIECE
SCALE = 1.0 / math.sqrt(NODES)
LIMIT = 40 * 2**20
WHOLE = 60 * 2**20
SWAP = [(0, 1), (1, 0)]


def contract_rows(left, right):
    return lax.dot_general(left, right, (((0,), (0,)), ((), ())), preferred_element_type=F32)


def split(value):
    high = value.astype(BF16)
    low = (value - high.astype(F32)).astype(BF16)
    return high, low


def pack_kernel(
    count_hbm, factor_hbm, side_hbm, cols_hbm, probe_hbm, pairs_hbm, rows_out, cols_out, count_ref, pairs_ref, sems
):
    copies = [
        pltpu.make_async_copy(source, target, sems.at[k])
        for k, (source, target) in enumerate(
            (
                (count_hbm, count_ref),
                (pairs_hbm, pairs_ref),
                (cols_hbm, cols_out.at[0, :, 0:RANK]),
                (probe_hbm, cols_out.at[0, :, RANK:WIDTH]),
                (factor_hbm, rows_out.at[0:BLOCK, 0:RANK]),
                (side_hbm, rows_out.at[0:BLOCK, RANK:WIDTH]),
            )
        )
    ]
    for copy in copies:
        copy.start()
    for copy in copies[:2]:
        copy.wait()
    slots = pairs_ref.shape[1]
    used = lax.broadcasted_iota(jnp.int32, (BLOCKS, slots), 1) < count_ref[0]
    same = lax.broadcasted_iota(jnp.int32, (BLOCKS, slots), 0) == pairs_ref[...]
    hits = jnp.where(same & used, 1.0, 0.0).astype(BF16)
    ones = jnp.ones((MASK_ROWS, slots), BF16)
    flags = lax.dot_general(ones, hits, (((1,), (1,)), ((), ())), preferred_element_type=F32)
    flags = jnp.concatenate([flags, jnp.zeros((MASK_ROWS, WIDTH - BLOCKS), F32)], 1)
    rows_out[BLOCK:LOAD_ROWS, :] = flags.astype(BF16)
    for copy in copies[2:4]:
        copy.wait()
    for s in range(1, Z):
        cols_out[s] = cols_out[0]
    for copy in copies[4:]:
        copy.wait()


def tile_kernel(rows0, rows1, rows2, rows3, low_ref, high_ref, row_ref, keep_ref, send_ref, row_acc, col_acc):
    y = lax.axis_index("y")
    core = lax.axis_index("c")
    gram = jnp.zeros((PROBES, 2 * PROBES), F32)
    for back, rows_ref in enumerate((rows0, rows1, rows2, rows3)):
        flags = 4.0 * rows_ref[BLOCK:LOAD_ROWS, 0:128].astype(F32)[0:8]
        for half in range(C):
            owner = core if half == 0 else 1 - core
            at = y * (Z * C) + owner
            turned = pltpu.roll(flags, lax.rem(128 - at, 128), 1)
            right = jnp.concatenate(
                [
                    (low_ref, high_ref)[s // 4][owner, s % 4, :, 0:RANK] * turned[0:1, C * s : C * s + 1].astype(BF16)
                    for s in range(Z)
                ],
                0,
            )
            right_probes = jnp.concatenate(
                [cols_ref[owner, :, :, RANK:WIDTH].reshape(HALF // 2, PROBES) for cols_ref in (low_ref, high_ref)], 0
            )
            scores = lax.dot_general(
                rows_ref[0:BLOCK, 0:RANK], right, (((1,), (1,)), ((), ())), preferred_element_type=F32
            )
            proximity = jnp.log(jnp.maximum(scores, 1.0)).astype(BF16)
            row_part = jnp.dot(proximity, right_probes, preferred_element_type=F32)
            if half == 0:
                row_acc[...] = row_part
            else:
                row_acc[...] += row_part
            col_part = contract_rows(rows_ref[0:BLOCK, RANK:WIDTH], proximity)
            if back == 0:
                col_acc[half] = col_part
            else:
                col_acc[half] += col_part
        high, low = split(row_acc[...])
        block = lax.rem(y + Y - back, Y)
        for q in range(X):
            row_ref[X * block + q] = high[SUB * q : SUB * (q + 1)]
        gram += contract_rows(rows_ref[0:BLOCK, RANK:WIDTH], jnp.concatenate([high, low], 1))
    for s in range(Z):
        keep_ref[s] = col_acc[0, :, s * SUB : (s + 1) * SUB]
        send_ref[s] = col_acc[1, :, s * SUB : (s + 1) * SUB]
    gram = gram[:, 0:PROBES] + gram[:, PROBES:]
    keep_ref[Z] = gram
    send_ref[Z] = gram


def join_kernel(keep_ref, got_ref, part_ref, rows_out, cols_out):
    for s in range(Z):
        cols_out[s, 0:SUB, :] = (keep_ref[s] + got_ref[s]).astype(BF16)
    core = lax.axis_index("c")
    half = PROBES // C
    at = pl.ds(pl.multiple_of(core * half, half), half)
    gram = keep_ref[Z, at, :] + got_ref[Z, at, :]
    high, low = split(gram)
    for y in range(Y):
        for x in range(X):
            rows_out[X * y + x, 0:SUB, :] = part_ref[X * y + x]
            rows_out[X * y + x, SUB : SUB + PIECE, :] = high[PIECE * x : PIECE * (x + 1)]
            rows_out[X * y + x, SUB + PIECE : SENT, :] = low[PIECE * x : PIECE * (x + 1)]


def row_kernel(got_ref, cols_ref, sketch_ref, cols_out):
    total = got_ref[0].astype(F32)
    for k in range(1, Y * X):
        total += got_ref[k].astype(F32)
    sketch_ref[...] = total[0:SUB] * SCALE
    high, low = split(total[SUB : SUB + PIECE] + total[SUB + PIECE : SENT])
    for s in range(Z):
        cols_out[s, 0:SUB, :] = cols_ref[s]
        cols_out[s, SUB : SUB + PIECE, :] = high
        cols_out[s, SUB + PIECE : SENT, :] = low


def col_kernel(got_ref, sketch_ref, gram_ref):
    total = got_ref[0].astype(F32)
    for k in range(1, Z):
        total += got_ref[k].astype(F32)
    sketch_ref[...] = total[0:SUB].T * SCALE
    gram_ref[...] = (total[SUB : SUB + PIECE] + total[SUB + PIECE : SENT]) * (1.0 / NODES)


def shards(factor_rows, row_side_probes, factor_cols, probe_cols, pair_blocks, pair_count):
    vmem = pl.BlockSpec(memory_space=pltpu.VMEM)
    hbm = pl.BlockSpec(memory_space=pl.ANY)
    params = pltpu.CompilerParams(vmem_limit_bytes=LIMIT)
    shape = jax.ShapeDtypeStruct

    row_load, col_load = pl.pallas_call(
        pack_kernel,
        out_shape=[shape((LOAD_ROWS, WIDTH), BF16), shape((Z, SUB, WIDTH), BF16)],
        in_specs=[hbm] * 6,
        out_specs=[vmem, vmem],
        scratch_shapes=[
            pltpu.SMEM((1,), jnp.int32),
            pltpu.VMEM(pair_blocks.shape, jnp.int32),
            pltpu.SemaphoreType.DMA((6,)),
        ],
        compiler_params=pltpu.CompilerParams(vmem_limit_bytes=WHOLE),
        name="pack",
    )(pair_count, factor_rows, row_side_probes, factor_cols, probe_cols, pair_blocks)
    all_rows = [row_load] + [lax.ppermute(row_load, "y", [(k, (k + s) % Y) for k in range(Y)]) for s in range(1, Y)]
    own_cols = lax.all_to_all(col_load, "z", split_axis=0, concat_axis=0, tiled=True)
    cols = [lax.all_gather(own_cols[k : k + Z // 2], "c", axis=0, tiled=False) for k in (0, Z // 2)]

    row_part, keep, send = pl.pallas_call(
        tile_kernel,
        out_shape=[
            shape((Y * X, SUB, PROBES), BF16),
            shape((Z + 1, PROBES, SUB), F32),
            shape((Z + 1, PROBES, SUB), F32),
        ],
        in_specs=[vmem] * 6,
        out_specs=[vmem, vmem, vmem],
        scratch_shapes=[
            pltpu.VMEM((BLOCK, PROBES), F32),
            pltpu.VMEM((C, PROBES, HALF), F32),
        ],
        compiler_params=params,
        name="tiles",
    )(*all_rows, *cols)

    got = lax.ppermute(send, "c", SWAP)
    row_load, col_part = pl.pallas_call(
        join_kernel,
        out_shape=[shape((Y * X, SENT, PROBES), BF16), shape((Z, SUB, SUB), BF16)],
        in_specs=[vmem, vmem, vmem],
        out_specs=[vmem, vmem],
        compiler_params=params,
        name="join",
    )(keep, got, row_part)
    row_got = lax.all_to_all(row_load, ("y", "x"), split_axis=0, concat_axis=0, tiled=True)
    row_sketch, col_load = pl.pallas_call(
        row_kernel,
        out_shape=[shape((SUB, PROBES), F32), shape((Z, SENT, SUB), BF16)],
        in_specs=[vmem, vmem],
        out_specs=[vmem, vmem],
        compiler_params=params,
        name="row_sum",
    )(row_got, col_part)
    col_got = lax.all_to_all(col_load, "z", split_axis=0, concat_axis=0, tiled=True)
    col_sketch, gram = pl.pallas_call(
        col_kernel,
        out_shape=[shape((SUB, PROBES), F32), shape((PIECE, PROBES), F32)],
        in_specs=[vmem],
        out_specs=[vmem, vmem],
        compiler_params=params,
        name="col_sum",
    )(col_got)

    x, c = lax.axis_index("x"), lax.axis_index("c")
    for axis, pairs, upper in (
        ("x", [(0, 1), (1, 0), (2, 3), (3, 2)], lax.rem(x, 2) == 1),
        ("x", [(0, 3), (3, 0), (1, 2), (2, 1)], x >= 2),
        ("c", SWAP, c == 1),
    ):
        peer = lax.ppermute(gram, axis, pairs)
        gram = jnp.concatenate([jnp.where(upper, peer, gram), jnp.where(upper, gram, peer)], 0)
    return (row_sketch, col_sketch, gram)


def solution(mesh):
    grid = Mesh(mesh.devices.reshape(Y, Z, C, X), ("y", "z", "c", "x"))
    rows, subs = ("y", "z", "c"), ("y", "z", "c", "x")
    return jax.shard_map(
        shards,
        mesh=grid,
        in_specs=(P(rows, None), P(rows, None), P(subs, None), P(subs, None), P(rows, None), P(rows)),
        out_specs=(P(subs, None), P(subs, None), P()),
        check_vma=False,
    )
```

```python
import math

import jax
import jax.numpy as jnp
from jax import lax
from jax.experimental import pallas as pl
from jax.experimental.pallas import tpu as pltpu
from jax.sharding import Mesh, PartitionSpec as P

BF16 = jnp.bfloat16
F32 = jnp.float32
Y, Z, C, X = 4, 8, 2, 4
BLOCKS = Y * Z * C
BLOCK, SUB, RANK, PROBES = 512, 128, 256, 128
WIDTH = RANK + PROBES
MASK_ROWS = 16
LOAD_ROWS = BLOCK + MASK_ROWS
HALF = Z * SUB
NODES = BLOCKS * BLOCK
PIECE = PROBES // (C * X)
SENT = SUB + 2 * PIECE
SCALE = 1.0 / math.sqrt(NODES)
LIMIT = 40 * 2**20
WHOLE = 60 * 2**20
SWAP = [(0, 1), (1, 0)]


def contract_rows(left, right):
    return lax.dot_general(left, right, (((0,), (0,)), ((), ())), preferred_element_type=F32)


def split(value):
    high = value.astype(BF16)
    low = (value - high.astype(F32)).astype(BF16)
    return high, low


def pack_kernel(
    count_hbm, factor_hbm, side_hbm, cols_hbm, probe_hbm, pairs_hbm, rows_out, cols_out, count_ref, pairs_ref, sems
):
    copies = [
        pltpu.make_async_copy(source, target, sems.at[k])
        for k, (source, target) in enumerate(
            (
                (count_hbm, count_ref),
                (pairs_hbm, pairs_ref),
                (cols_hbm, cols_out.at[0, :, 0:RANK]),
                (probe_hbm, cols_out.at[0, :, RANK:WIDTH]),
                (factor_hbm, rows_out.at[0:BLOCK, 0:RANK]),
                (side_hbm, rows_out.at[0:BLOCK, RANK:WIDTH]),
            )
        )
    ]
    for copy in copies:
        copy.start()
    for copy in copies[:2]:
        copy.wait()
    slots = pairs_ref.shape[1]
    used = lax.broadcasted_iota(jnp.int32, (BLOCKS, slots), 1) < count_ref[0]
    same = lax.broadcasted_iota(jnp.int32, (BLOCKS, slots), 0) == pairs_ref[...]
    hits = jnp.where(same & used, 1.0, 0.0).astype(BF16)
    ones = jnp.ones((MASK_ROWS, slots), BF16)
    flags = lax.dot_general(ones, hits, (((1,), (1,)), ((), ())), preferred_element_type=F32)
    flags = jnp.concatenate([flags, jnp.zeros((MASK_ROWS, WIDTH - BLOCKS), F32)], 1)
    rows_out[BLOCK:LOAD_ROWS, :] = flags.astype(BF16)
    for copy in copies[2:4]:
        copy.wait()
    for s in range(1, Z):
        cols_out[s] = cols_out[0]
    for copy in copies[4:]:
        copy.wait()


def tiles(shift, rows_refs, cols_refs, row_acc, first, col_acc):
    owner = lax.axis_index("c") if shift == 0 else 1 - lax.axis_index("c")
    at = lax.axis_index("y") * (Z * C) + owner
    subs = [cols_ref.at[s] for cols_ref in cols_refs for s in range(cols_ref.shape[0])]
    right_probes = jnp.concatenate([sub[:, RANK:WIDTH] for sub in subs], 0)
    for back, rows_ref in enumerate(rows_refs):
        flags = 4.0 * rows_ref[BLOCK:LOAD_ROWS, 0:128].astype(F32)[0:8]
        turned = pltpu.roll(flags, lax.rem(128 - at, 128), 1)
        right = jnp.concatenate(
            [sub[:, 0:RANK] * turned[0:1, C * s : C * s + 1].astype(BF16) for s, sub in enumerate(subs)], 0
        )
        scores = lax.dot_general(
            rows_ref[0:BLOCK, 0:RANK], right, (((1,), (1,)), ((), ())), preferred_element_type=F32
        )
        proximity = jnp.log(jnp.maximum(scores, 1.0)).astype(BF16)
        row_part = jnp.dot(proximity, right_probes, preferred_element_type=F32)
        row_acc[back] = row_part if first is None else first[back] + row_part
        col_part = contract_rows(rows_ref[0:BLOCK, RANK:WIDTH], proximity)
        if back == 0:
            col_acc[...] = col_part
        else:
            col_acc[...] += col_part
    gram = jnp.dot(jnp.concatenate(split(col_acc[...]), 0), right_probes, preferred_element_type=F32)
    return gram[0:PROBES] + gram[PROBES:]


def own_kernel(rows0, rows1, rows2, rows3, low_ref, high_ref, row_ref, keep_ref, gram_ref, col_acc):
    gram_ref[...] = tiles(0, (rows0, rows1, rows2, rows3), (low_ref, high_ref), row_ref, None, col_acc)
    for s in range(Z):
        keep_ref[s] = col_acc[:, s * SUB : (s + 1) * SUB]


def other_kernel(rows0, rows1, rows2, rows3, low_ref, high_ref, first_ref, gram_ref, row_ref, send_ref, row_acc, col_acc):
    gram = tiles(1, (rows0, rows1, rows2, rows3), (low_ref, high_ref), row_acc, first_ref, col_acc)
    y = lax.axis_index("y")
    for back in range(Y):
        block = lax.rem(y + Y - back, Y)
        for q in range(X):
            row_ref[X * block + q] = row_acc[back, SUB * q : SUB * (q + 1)].astype(BF16)
    for s in range(Z):
        send_ref[s] = col_acc[:, s * SUB : (s + 1) * SUB]
    send_ref[Z] = gram_ref[...] + gram


def join_kernel(keep_ref, sent_ref, got_ref, part_ref, rows_out, cols_out):
    for s in range(Z):
        cols_out[s, 0:SUB, :] = (keep_ref[s] + got_ref[s]).astype(BF16)
    core = lax.axis_index("c")
    half = PROBES // C
    at = pl.ds(pl.multiple_of(core * half, half), half)
    gram = sent_ref[Z, at, :] + got_ref[Z, at, :]
    high, low = split(gram)
    for y in range(Y):
        for x in range(X):
            rows_out[X * y + x, 0:SUB, :] = part_ref[X * y + x]
            rows_out[X * y + x, SUB : SUB + PIECE, :] = high[PIECE * x : PIECE * (x + 1)]
            rows_out[X * y + x, SUB + PIECE : SENT, :] = low[PIECE * x : PIECE * (x + 1)]


def row_kernel(got_ref, cols_ref, sketch_ref, cols_out):
    total = got_ref[0].astype(F32)
    for k in range(1, Y * X):
        total += got_ref[k].astype(F32)
    sketch_ref[...] = total[0:SUB] * SCALE
    high, low = split(total[SUB : SUB + PIECE] + total[SUB + PIECE : SENT])
    for s in range(Z):
        cols_out[s, 0:SUB, :] = cols_ref[s]
        cols_out[s, SUB : SUB + PIECE, :] = high
        cols_out[s, SUB + PIECE : SENT, :] = low


def col_kernel(got_ref, sketch_ref, gram_ref):
    total = got_ref[0].astype(F32)
    for k in range(1, Z):
        total += got_ref[k].astype(F32)
    sketch_ref[...] = total[0:SUB].T * SCALE
    gram_ref[...] = (total[SUB : SUB + PIECE] + total[SUB + PIECE : SENT]) * (1.0 / NODES)


def shards(factor_rows, row_side_probes, factor_cols, probe_cols, pair_blocks, pair_count):
    vmem = pl.BlockSpec(memory_space=pltpu.VMEM)
    hbm = pl.BlockSpec(memory_space=pl.ANY)
    params = pltpu.CompilerParams(vmem_limit_bytes=LIMIT)
    shape = jax.ShapeDtypeStruct

    row_load, col_load = pl.pallas_call(
        pack_kernel,
        out_shape=[shape((LOAD_ROWS, WIDTH), BF16), shape((Z, SUB, WIDTH), BF16)],
        in_specs=[hbm] * 6,
        out_specs=[vmem, vmem],
        scratch_shapes=[
            pltpu.SMEM((1,), jnp.int32),
            pltpu.VMEM(pair_blocks.shape, jnp.int32),
            pltpu.SemaphoreType.DMA((6,)),
        ],
        compiler_params=pltpu.CompilerParams(vmem_limit_bytes=WHOLE),
        name="pack",
    )(pair_count, factor_rows, row_side_probes, factor_cols, probe_cols, pair_blocks)
    all_rows = [row_load] + [lax.ppermute(row_load, "y", [(k, (k + s) % Y) for k in range(Y)]) for s in range(1, Y)]
    own_cols = lax.all_to_all(col_load, "z", split_axis=0, concat_axis=0, tiled=True)
    own_cols = [own_cols[: Z // 2], own_cols[Z // 2 :]]
    other_cols = [lax.ppermute(part, "c", SWAP) for part in own_cols]

    cost = pl.CostEstimate(
        flops=2 * Y * BLOCK * HALF * (RANK + 2 * PROBES), bytes_accessed=4 * 2**20, transcendentals=Y * BLOCK * HALF
    )
    first, keep, gram = pl.pallas_call(
        own_kernel,
        out_shape=[shape((Y, BLOCK, PROBES), F32), shape((Z, PROBES, SUB), F32), shape((PROBES, PROBES), F32)],
        in_specs=[vmem] * 6,
        out_specs=[vmem] * 3,
        scratch_shapes=[pltpu.VMEM((PROBES, HALF), F32)],
        compiler_params=params,
        cost_estimate=cost,
        name="own_tiles",
    )(*all_rows, *own_cols)
    row_part, send = pl.pallas_call(
        other_kernel,
        out_shape=[shape((Y * X, SUB, PROBES), BF16), shape((Z + 1, PROBES, SUB), F32)],
        in_specs=[vmem] * 8,
        out_specs=[vmem] * 2,
        scratch_shapes=[pltpu.VMEM((Y, BLOCK, PROBES), F32), pltpu.VMEM((PROBES, HALF), F32)],
        compiler_params=params,
        cost_estimate=cost,
        name="other_tiles",
    )(*all_rows, *other_cols, first, gram)

    got = lax.ppermute(send, "c", SWAP)
    row_load, col_part = pl.pallas_call(
        join_kernel,
        out_shape=[shape((Y * X, SENT, PROBES), BF16), shape((Z, SUB, SUB), BF16)],
        in_specs=[vmem] * 4,
        out_specs=[vmem, vmem],
        compiler_params=params,
        name="join",
    )(keep, send, got, row_part)
    row_got = lax.all_to_all(row_load, ("y", "x"), split_axis=0, concat_axis=0, tiled=True)
    row_sketch, col_load = pl.pallas_call(
        row_kernel,
        out_shape=[shape((SUB, PROBES), F32), shape((Z, SENT, SUB), BF16)],
        in_specs=[vmem, vmem],
        out_specs=[vmem, vmem],
        compiler_params=params,
        name="row_sum",
    )(row_got, col_part)
    col_got = lax.all_to_all(col_load, "z", split_axis=0, concat_axis=0, tiled=True)
    col_sketch, gram = pl.pallas_call(
        col_kernel,
        out_shape=[shape((SUB, PROBES), F32), shape((PIECE, PROBES), F32)],
        in_specs=[vmem],
        out_specs=[vmem, vmem],
        compiler_params=params,
        name="col_sum",
    )(col_got)

    x, c = lax.axis_index("x"), lax.axis_index("c")
    for axis, pairs, upper in (
        ("x", [(0, 1), (1, 0), (2, 3), (3, 2)], lax.rem(x, 2) == 1),
        ("x", [(0, 3), (3, 0), (1, 2), (2, 1)], x >= 2),
        ("c", SWAP, c == 1),
    ):
        peer = lax.ppermute(gram, axis, pairs)
        gram = jnp.concatenate([jnp.where(upper, peer, gram), jnp.where(upper, gram, peer)], 0)
    return (row_sketch, col_sketch, gram)


def solution(mesh):
    grid = Mesh(mesh.devices.reshape(Y, Z, C, X), ("y", "z", "c", "x"))
    rows, subs = ("y", "z", "c"), ("y", "z", "c", "x")
    return jax.shard_map(
        shards,
        mesh=grid,
        in_specs=(P(rows, None), P(rows, None), P(subs, None), P(subs, None), P(rows, None), P(rows)),
        out_specs=(P(subs, None), P(subs, None), P()),
        check_vma=False,
    )
```

```python
import math

import jax
import jax.numpy as jnp
from jax import lax
from jax.experimental import pallas as pl
from jax.experimental.pallas import tpu as pltpu
from jax.sharding import Mesh, PartitionSpec as P

BF16 = jnp.bfloat16
F32 = jnp.float32
Y, Z, C, X = 4, 8, 2, 4
BLOCKS = Y * Z * C
BLOCK, SUB, RANK, PROBES = 512, 128, 256, 128
WIDTH = RANK + PROBES
MASK_ROWS = 16
LOAD_ROWS = BLOCK + MASK_ROWS
HALF = Z * SUB
NODES = BLOCKS * BLOCK
TERMS = 1
SENT = SUB + TERMS * PROBES // C
SCALE = 1.0 / math.sqrt(NODES)
LIMIT = 40 * 2**20
WHOLE = 60 * 2**20
SWAP = [(0, 1), (1, 0)]


def ring(size, shift):
    return [(k, (k + shift) % size) for k in range(size)]


def contract_rows(left, right):
    return lax.dot_general(left, right, (((0,), (0,)), ((), ())), preferred_element_type=F32)


def split(value):
    high = value.astype(BF16)
    low = (value - high.astype(F32)).astype(BF16)
    return high, low


def pack_kernel(
    count_hbm, factor_hbm, side_hbm, cols_hbm, probe_hbm, pairs_hbm, rows_out, cols_out, count_ref, pairs_ref, sems
):
    copies = [
        pltpu.make_async_copy(source, target, sems.at[k])
        for k, (source, target) in enumerate(
            (
                (count_hbm, count_ref),
                (pairs_hbm, pairs_ref),
                (cols_hbm, cols_out.at[0, :, 0:RANK]),
                (probe_hbm, cols_out.at[0, :, RANK:WIDTH]),
                (factor_hbm, rows_out.at[0:BLOCK, 0:RANK]),
                (side_hbm, rows_out.at[0:BLOCK, RANK:WIDTH]),
            )
        )
    ]
    for copy in copies:
        copy.start()
    for copy in copies[:2]:
        copy.wait()
    slots = pairs_ref.shape[1]
    used = lax.broadcasted_iota(jnp.int32, (BLOCKS, slots), 1) < count_ref[0]
    same = lax.broadcasted_iota(jnp.int32, (BLOCKS, slots), 0) == pairs_ref[...]
    hits = jnp.where(same & used, 1.0, 0.0).astype(BF16)
    ones = jnp.ones((MASK_ROWS, slots), BF16)
    flags = lax.dot_general(ones, hits, (((1,), (1,)), ((), ())), preferred_element_type=F32)
    flags = jnp.concatenate([flags, jnp.zeros((MASK_ROWS, WIDTH - BLOCKS), F32)], 1)
    rows_out[BLOCK:LOAD_ROWS, :] = flags.astype(BF16)
    for copy in copies[2:4]:
        copy.wait()
    for s in range(1, Z):
        cols_out[s] = cols_out[0]
    for copy in copies[4:]:
        copy.wait()


def tiles(shift, rows_refs, cols_refs, row_acc, first, col_acc):
    owner = lax.axis_index("c") if shift == 0 else 1 - lax.axis_index("c")
    at = lax.axis_index("y") * (Z * C) + owner
    subs = [cols_ref.at[s] for cols_ref in cols_refs for s in range(cols_ref.shape[0])]
    right_probes = jnp.concatenate([sub[:, RANK:WIDTH] for sub in subs], 0)
    for back, rows_ref in enumerate(rows_refs):
        flags = 4.0 * rows_ref[BLOCK:LOAD_ROWS, 0:128].astype(F32)[0:8]
        turned = pltpu.roll(flags, lax.rem(128 - at, 128), 1)
        right = jnp.concatenate(
            [sub[:, 0:RANK] * turned[0:1, C * s : C * s + 1].astype(BF16) for s, sub in enumerate(subs)], 0
        )
        scores = lax.dot_general(
            rows_ref[0:BLOCK, 0:RANK], right, (((1,), (1,)), ((), ())), preferred_element_type=F32
        )
        proximity = jnp.log(jnp.maximum(scores, 1.0)).astype(BF16)
        row_part = jnp.dot(proximity, right_probes, preferred_element_type=F32)
        row_acc[back] = row_part if first is None else first[back] + row_part
        col_part = contract_rows(rows_ref[0:BLOCK, RANK:WIDTH], proximity)
        if back == 0:
            col_acc[...] = col_part
        else:
            col_acc[...] += col_part
    gram = jnp.dot(jnp.concatenate(split(col_acc[...]), 0), right_probes, preferred_element_type=F32)
    return gram[0:PROBES] + gram[PROBES:]


def own_kernel(rows0, rows1, rows2, rows3, low_ref, high_ref, row_ref, keep_ref, gram_ref, col_acc):
    gram_ref[...] = tiles(0, (rows0, rows1, rows2, rows3), (low_ref, high_ref), row_ref, None, col_acc)
    for s in range(Z):
        keep_ref[s] = col_acc[:, s * SUB : (s + 1) * SUB]


def other_kernel(
    rows0, rows1, rows2, rows3, low_ref, high_ref, first_ref, gram_ref, piece0, piece1, piece2, piece3, send_ref, row_acc, col_acc
):
    gram = tiles(1, (rows0, rows1, rows2, rows3), (low_ref, high_ref), row_acc, first_ref, col_acc)
    x = lax.axis_index("x")
    for ahead, piece in enumerate((piece0, piece1, piece2, piece3)):
        at = pl.ds(pl.multiple_of(SUB * lax.rem(x + ahead, X), SUB), SUB)
        for back in range(Y):
            piece[back] = row_acc[back, at, :].astype(piece.dtype)
    for s in range(Z):
        send_ref[s] = col_acc[:, s * SUB : (s + 1) * SUB]
    send_ref[Z] = gram_ref[...] + gram


def join_kernel(keep_ref, sent_ref, got_ref, cols_out):
    half = PROBES // C
    at = pl.ds(pl.multiple_of(lax.axis_index("c") * half, half), half)
    parts = split(sent_ref[Z, at, :] + got_ref[Z, at, :])
    for s in range(Z):
        cols_out[s, 0:SUB, :] = (keep_ref[s] + got_ref[s]).astype(BF16)
        for k in range(TERMS):
            cols_out[s, SUB + half * k : SUB + half * (k + 1), :] = parts[k]


def piece_kernel(kept_ref, got1, got2, got3, col_ref, out0, out1, out2, out3, gram_out):
    half = PROBES // C
    gram = col_ref[SUB : SUB + half]
    for k in range(1, TERMS):
        gram += col_ref[SUB + half * k : SUB + half * (k + 1)]
    for k in range(Y * X):
        gram_out[k] = gram
    for back, out in enumerate((out0, out1, out2, out3)):
        total = kept_ref[back]
        for got in (got1, got2, got3):
            total += got[back].astype(F32)
        out[...] = total


def shards(factor_rows, row_side_probes, factor_cols, probe_cols, pair_blocks, pair_count):
    vmem = pl.BlockSpec(memory_space=pltpu.VMEM)
    hbm = pl.BlockSpec(memory_space=pl.ANY)
    params = pltpu.CompilerParams(vmem_limit_bytes=LIMIT)
    shape = jax.ShapeDtypeStruct

    row_load, col_load = pl.pallas_call(
        pack_kernel,
        out_shape=[shape((LOAD_ROWS, WIDTH), BF16), shape((Z, SUB, WIDTH), BF16)],
        in_specs=[hbm] * 6,
        out_specs=[vmem, vmem],
        scratch_shapes=[
            pltpu.SMEM((1,), jnp.int32),
            pltpu.VMEM(pair_blocks.shape, jnp.int32),
            pltpu.SemaphoreType.DMA((6,)),
        ],
        compiler_params=pltpu.CompilerParams(vmem_limit_bytes=WHOLE),
        name="pack",
    )(pair_count, factor_rows, row_side_probes, factor_cols, probe_cols, pair_blocks)
    all_rows = [row_load] + [lax.ppermute(row_load, "y", ring(Y, s)) for s in range(1, Y)]
    own_cols = lax.all_to_all(col_load, "z", split_axis=0, concat_axis=0, tiled=True)
    own_cols = [own_cols[: Z // 2], own_cols[Z // 2 :]]
    other_cols = [lax.ppermute(part, "c", SWAP) for part in own_cols]

    cost = pl.CostEstimate(
        flops=2 * Y * BLOCK * HALF * (RANK + 2 * PROBES), bytes_accessed=4 * 2**20, transcendentals=Y * BLOCK * HALF
    )
    first, keep, gram = pl.pallas_call(
        own_kernel,
        out_shape=[shape((Y, BLOCK, PROBES), F32), shape((Z, PROBES, SUB), F32), shape((PROBES, PROBES), F32)],
        in_specs=[vmem] * 6,
        out_specs=[vmem] * 3,
        scratch_shapes=[pltpu.VMEM((PROBES, HALF), F32)],
        compiler_params=params,
        cost_estimate=cost,
        name="own_tiles",
    )(*all_rows, *own_cols)
    *pieces, send = pl.pallas_call(
        other_kernel,
        out_shape=[shape((Y, SUB, PROBES), F32)]
        + [shape((Y, SUB, PROBES), BF16)] * (X - 1)
        + [shape((Z + 1, PROBES, SUB), F32)],
        in_specs=[vmem] * 8,
        out_specs=[vmem] * 5,
        scratch_shapes=[pltpu.VMEM((Y, BLOCK, PROBES), F32), pltpu.VMEM((PROBES, HALF), F32)],
        compiler_params=params,
        cost_estimate=cost,
        name="other_tiles",
    )(*all_rows, *other_cols, first, gram)

    got = lax.ppermute(send, "c", SWAP)
    got_pieces = [lax.ppermute(pieces[s], "x", ring(X, s)) for s in range(1, X)]
    col_load = pl.pallas_call(
        join_kernel,
        out_shape=shape((Z, SENT, SUB), BF16),
        in_specs=[vmem] * 3,
        out_specs=vmem,
        compiler_params=params,
        name="join",
    )(keep, send, got)
    col_got = lax.all_to_all(col_load, "z", split_axis=0, concat_axis=0, tiled=True)
    col_sum = jnp.sum(col_got.astype(F32), 0)
    half = PROBES // C
    col_sketch = col_sum[:SUB].T * SCALE

    *sums, gram = pl.pallas_call(
        piece_kernel,
        out_shape=[shape((SUB, PROBES), F32)] * Y + [shape((Y * X, half, PROBES), F32)],
        in_specs=[vmem] * 5,
        out_specs=[vmem] * 5,
        compiler_params=params,
        name="pieces",
    )(pieces[0], *got_pieces, col_sum)
    got_sums = [lax.ppermute(sums[back], "y", ring(Y, Y - back)) for back in range(1, Y)]
    row_sketch = (sums[0] + got_sums[0] + got_sums[1] + got_sums[2]) * SCALE

    gram = lax.all_to_all(gram, ("y", "x"), split_axis=0, concat_axis=0, tiled=True)
    gram = jnp.sum(gram, 0) * (1.0 / NODES)
    peer = lax.ppermute(gram, "c", SWAP)
    upper = lax.axis_index("c") == 1
    sketch_gram = jnp.concatenate([jnp.where(upper, peer, gram), jnp.where(upper, gram, peer)], 0)
    return (row_sketch, col_sketch, sketch_gram)


def solution(mesh):
    grid = Mesh(mesh.devices.reshape(Y, Z, C, X), ("y", "z", "c", "x"))
    rows, subs = ("y", "z", "c"), ("y", "z", "c", "x")
    return jax.shard_map(
        shards,
        mesh=grid,
        in_specs=(P(rows, None), P(rows, None), P(subs, None), P(subs, None), P(rows, None), P(rows)),
        out_specs=(P(subs, None), P(subs, None), P()),
        check_vma=False,
    )
```

```python
import math

import jax
import jax.numpy as jnp
from jax import lax
from jax.experimental import pallas as pl
from jax.experimental.pallas import tpu as pltpu
from jax.sharding import Mesh, PartitionSpec as P

BF16 = jnp.bfloat16
F32 = jnp.float32
Y, Z, C, X = 4, 8, 2, 4
BLOCKS = Y * Z * C
BLOCK, SUB, RANK, PROBES = 512, 128, 256, 128
WIDTH = RANK + PROBES
MASK_ROWS = 16
LOAD_ROWS = BLOCK + MASK_ROWS
HALF = Z * SUB
CUT = 272
NODES = BLOCKS * BLOCK
TERMS = 1
SENT = SUB + TERMS * PROBES // C
SCALE = 1.0 / math.sqrt(NODES)
LIMIT = 40 * 2**20
WHOLE = 60 * 2**20
SWAP = [(0, 1), (1, 0)]


def ring(size, shift):
    return [(k, (k + shift) % size) for k in range(size)]


def contract_rows(left, right):
    return lax.dot_general(left, right, (((0,), (0,)), ((), ())), preferred_element_type=F32)


def split(value):
    high = value.astype(BF16)
    low = (value - high.astype(F32)).astype(BF16)
    return high, low


def pack_kernel(
    count_hbm, factor_hbm, side_hbm, cols_hbm, probe_hbm, pairs_hbm, rows_out, cols_out, count_ref, pairs_ref, sems
):
    copies = [
        pltpu.make_async_copy(source, target, sems.at[k])
        for k, (source, target) in enumerate(
            (
                (count_hbm, count_ref),
                (pairs_hbm, pairs_ref),
                (cols_hbm, cols_out.at[0, :, 0:RANK]),
                (probe_hbm, cols_out.at[0, :, RANK:WIDTH]),
                (factor_hbm, rows_out.at[0:BLOCK, 0:RANK]),
                (side_hbm, rows_out.at[0:BLOCK, RANK:WIDTH]),
            )
        )
    ]
    for copy in copies:
        copy.start()
    for copy in copies[:2]:
        copy.wait()
    slots = pairs_ref.shape[1]
    used = lax.broadcasted_iota(jnp.int32, (BLOCKS, slots), 1) < count_ref[0]
    same = lax.broadcasted_iota(jnp.int32, (BLOCKS, slots), 0) == pairs_ref[...]
    hits = jnp.where(same & used, 1.0, 0.0).astype(BF16)
    ones = jnp.ones((MASK_ROWS, slots), BF16)
    flags = lax.dot_general(ones, hits, (((1,), (1,)), ((), ())), preferred_element_type=F32)
    flags = jnp.concatenate([flags, jnp.zeros((MASK_ROWS, WIDTH - BLOCKS), F32)], 1)
    rows_out[BLOCK:LOAD_ROWS, :] = flags.astype(BF16)
    for copy in copies[2:4]:
        copy.wait()
    for s in range(1, Z):
        cols_out[s] = cols_out[0]
    for copy in copies[4:]:
        copy.wait()


def tiles(shift, rows_refs, cols_refs, row_acc, first, col_acc):
    owner = lax.axis_index("c") if shift == 0 else 1 - lax.axis_index("c")
    at = lax.axis_index("y") * (Z * C) + owner
    subs = [cols_ref.at[s] for cols_ref in cols_refs for s in range(cols_ref.shape[0])]
    right_probes = jnp.concatenate([sub[:, RANK:WIDTH] for sub in subs], 0)
    rows0, rows1, far_low, far_high, rows3 = rows_refs
    for back, parts in enumerate(((rows0,), (rows1,), (far_low, far_high), (rows3,))):
        loads = [part[...] for part in parts]
        whole = loads[0] if len(loads) == 1 else jnp.concatenate(loads, 0)
        left, left_probes = whole[0:BLOCK, 0:RANK], whole[0:BLOCK, RANK:WIDTH]
        flags = 4.0 * whole[BLOCK:LOAD_ROWS, 0:128].astype(F32)[0:8]
        turned = pltpu.roll(flags, lax.rem(128 - at, 128), 1)
        right = jnp.concatenate(
            [sub[:, 0:RANK] * turned[0:1, C * s : C * s + 1].astype(BF16) for s, sub in enumerate(subs)], 0
        )
        scores = lax.dot_general(
            left, right, (((1,), (1,)), ((), ())), preferred_element_type=F32
        )
        proximity = jnp.log(jnp.maximum(scores, 1.0)).astype(BF16)
        row_part = jnp.dot(proximity, right_probes, preferred_element_type=F32)
        row_acc[back] = row_part if first is None else first[back] + row_part
        col_part = contract_rows(left_probes, proximity)
        if back == 0:
            col_acc[...] = col_part
        else:
            col_acc[...] += col_part
    gram = jnp.dot(jnp.concatenate(split(col_acc[...]), 0), right_probes, preferred_element_type=F32)
    return gram[0:PROBES] + gram[PROBES:]


def own_kernel(rows0, rows1, far_low, far_high, rows3, low_ref, high_ref, row_ref, keep_ref, gram_ref, col_acc):
    gram_ref[...] = tiles(0, (rows0, rows1, far_low, far_high, rows3), (low_ref, high_ref), row_ref, None, col_acc)
    for s in range(Z):
        keep_ref[s] = col_acc[:, s * SUB : (s + 1) * SUB]


def other_kernel(
    rows0, rows1, far_low, far_high, rows3, low_ref, high_ref, first_ref, gram_ref, piece0, piece1, piece2, piece3, send_ref, row_acc, col_acc
):
    gram = tiles(1, (rows0, rows1, far_low, far_high, rows3), (low_ref, high_ref), row_acc, first_ref, col_acc)
    x = lax.axis_index("x")
    for ahead, piece in enumerate((piece0, piece1, piece2, piece3)):
        at = pl.ds(pl.multiple_of(SUB * lax.rem(x + ahead, X), SUB), SUB)
        for back in range(Y):
            piece[back] = row_acc[back, at, :].astype(piece.dtype)
    for s in range(Z):
        send_ref[s] = col_acc[:, s * SUB : (s + 1) * SUB]
    send_ref[Z] = gram_ref[...] + gram


def join_kernel(keep_ref, sent_ref, got_ref, cols_out):
    half = PROBES // C
    at = pl.ds(pl.multiple_of(lax.axis_index("c") * half, half), half)
    parts = split(sent_ref[Z, at, :] + got_ref[Z, at, :])
    for s in range(Z):
        cols_out[s, 0:SUB, :] = (keep_ref[s] + got_ref[s]).astype(BF16)
        for k in range(TERMS):
            cols_out[s, SUB + half * k : SUB + half * (k + 1), :] = parts[k]


def piece_kernel(kept_ref, got1, got2, got3, col_ref, out0, out1, out2, out3, gram_out):
    half = PROBES // C
    gram = col_ref[SUB : SUB + half]
    for k in range(1, TERMS):
        gram += col_ref[SUB + half * k : SUB + half * (k + 1)]
    for k in range(Y * X):
        gram_out[k] = gram
    for back, out in enumerate((out0, out1, out2, out3)):
        total = kept_ref[back]
        for got in (got1, got2, got3):
            total += got[back].astype(F32)
        out[...] = total


def shards(factor_rows, row_side_probes, factor_cols, probe_cols, pair_blocks, pair_count):
    vmem = pl.BlockSpec(memory_space=pltpu.VMEM)
    hbm = pl.BlockSpec(memory_space=pl.ANY)
    params = pltpu.CompilerParams(vmem_limit_bytes=LIMIT)
    shape = jax.ShapeDtypeStruct

    row_load, col_load = pl.pallas_call(
        pack_kernel,
        out_shape=[shape((LOAD_ROWS, WIDTH), BF16), shape((Z, SUB, WIDTH), BF16)],
        in_specs=[hbm] * 6,
        out_specs=[vmem, vmem],
        scratch_shapes=[
            pltpu.SMEM((1,), jnp.int32),
            pltpu.VMEM(pair_blocks.shape, jnp.int32),
            pltpu.SemaphoreType.DMA((6,)),
        ],
        compiler_params=pltpu.CompilerParams(vmem_limit_bytes=WHOLE),
        name="pack",
    )(pair_count, factor_rows, row_side_probes, factor_cols, probe_cols, pair_blocks)
    near = [lax.ppermute(row_load, "y", ring(Y, s)) for s in (1, 3)]
    far = [lax.ppermute(near[0][:CUT], "y", ring(Y, 1)), lax.ppermute(near[1][CUT:], "y", ring(Y, 3))]
    all_rows = [row_load, near[0], *far, near[1]]
    own_cols = lax.all_to_all(col_load, "z", split_axis=0, concat_axis=0, tiled=True)
    own_cols = [own_cols[: Z // 2], own_cols[Z // 2 :]]
    other_cols = [lax.ppermute(part, "c", SWAP) for part in own_cols]

    cost = pl.CostEstimate(
        flops=2 * Y * BLOCK * HALF * (RANK + 2 * PROBES), bytes_accessed=4 * 2**20, transcendentals=Y * BLOCK * HALF
    )
    first, keep, gram = pl.pallas_call(
        own_kernel,
        out_shape=[shape((Y, BLOCK, PROBES), F32), shape((Z, PROBES, SUB), F32), shape((PROBES, PROBES), F32)],
        in_specs=[vmem] * 7,
        out_specs=[vmem] * 3,
        scratch_shapes=[pltpu.VMEM((PROBES, HALF), F32)],
        compiler_params=params,
        cost_estimate=cost,
        name="own_tiles",
    )(*all_rows, *own_cols)
    *pieces, send = pl.pallas_call(
        other_kernel,
        out_shape=[shape((Y, SUB, PROBES), F32)]
        + [shape((Y, SUB, PROBES), BF16)] * (X - 1)
        + [shape((Z + 1, PROBES, SUB), F32)],
        in_specs=[vmem] * 9,
        out_specs=[vmem] * 5,
        scratch_shapes=[pltpu.VMEM((Y, BLOCK, PROBES), F32), pltpu.VMEM((PROBES, HALF), F32)],
        compiler_params=params,
        cost_estimate=cost,
        name="other_tiles",
    )(*all_rows, *other_cols, first, gram)

    got = lax.ppermute(send, "c", SWAP)
    got_pieces = [lax.ppermute(pieces[s], "x", ring(X, s)) for s in range(1, X)]
    col_load = pl.pallas_call(
        join_kernel,
        out_shape=shape((Z, SENT, SUB), BF16),
        in_specs=[vmem] * 3,
        out_specs=vmem,
        compiler_params=params,
        name="join",
    )(keep, send, got)
    col_got = lax.all_to_all(col_load, "z", split_axis=0, concat_axis=0, tiled=True)
    col_sum = jnp.sum(col_got.astype(F32), 0)
    half = PROBES // C
    col_sketch = col_sum[:SUB].T * SCALE

    *sums, gram = pl.pallas_call(
        piece_kernel,
        out_shape=[shape((SUB, PROBES), F32)] * Y + [shape((Y * X, half, PROBES), F32)],
        in_specs=[vmem] * 5,
        out_specs=[vmem] * 5,
        compiler_params=params,
        name="pieces",
    )(pieces[0], *got_pieces, col_sum)
    got_sums = [lax.ppermute(sums[back], "y", ring(Y, Y - back)) for back in range(1, Y)]
    row_sketch = (sums[0] + got_sums[0] + got_sums[1] + got_sums[2]) * SCALE

    gram = lax.all_to_all(gram, ("y", "x"), split_axis=0, concat_axis=0, tiled=True)
    gram = jnp.sum(gram, 0) * (1.0 / NODES)
    peer = lax.ppermute(gram, "c", SWAP)
    upper = lax.axis_index("c") == 1
    sketch_gram = jnp.concatenate([jnp.where(upper, peer, gram), jnp.where(upper, gram, peer)], 0)
    return (row_sketch, col_sketch, sketch_gram)


def solution(mesh):
    grid = Mesh(mesh.devices.reshape(Y, Z, C, X), ("y", "z", "c", "x"))
    rows, subs = ("y", "z", "c"), ("y", "z", "c", "x")
    return jax.shard_map(
        shards,
        mesh=grid,
        in_specs=(P(rows, None), P(rows, None), P(subs, None), P(subs, None), P(rows, None), P(rows)),
        out_specs=(P(subs, None), P(subs, None), P()),
        check_vma=False,
    )
```

```python
import math

import jax
import jax.numpy as jnp
from jax import lax
from jax.experimental import pallas as pl
from jax.experimental.pallas import tpu as pltpu
from jax.sharding import Mesh, PartitionSpec as P

BF16 = jnp.bfloat16
F32 = jnp.float32
Y, Z, C, X = 4, 8, 2, 4
BLOCKS = Y * Z * C
BLOCK, SUB, RANK, PROBES = 512, 128, 256, 128
WIDTH = RANK + PROBES
MASK_ROWS = 16
LOAD_ROWS = BLOCK + MASK_ROWS
HALF = Z * SUB
CUT = 272
NODES = BLOCKS * BLOCK
TERMS = 1
SENT = SUB + TERMS * PROBES // C
SCALE = 1.0 / math.sqrt(NODES)
LIMIT = 40 * 2**20
WHOLE = 60 * 2**20
SWAP = [(0, 1), (1, 0)]


def ring(size, shift):
    return [(k, (k + shift) % size) for k in range(size)]


def contract_rows(left, right):
    return lax.dot_general(left, right, (((0,), (0,)), ((), ())), preferred_element_type=F32)


def split(value):
    high = value.astype(BF16)
    low = (value - high.astype(F32)).astype(BF16)
    return high, low


def pack_kernel(
    count_hbm, factor_hbm, side_hbm, cols_hbm, probe_hbm, pairs_hbm,
    rows_out, cols_out, count_ref, pairs_ref, cols_ref, rows_ref, sems, out_sems
):
    pairs = (
        (cols_hbm, cols_ref.at[:, 0:RANK]),
        (probe_hbm, cols_ref.at[:, RANK:WIDTH]),
        (count_hbm, count_ref),
        (pairs_hbm, pairs_ref),
        (factor_hbm, rows_ref.at[0:BLOCK, 0:RANK]),
        (side_hbm, rows_ref.at[0:BLOCK, RANK:WIDTH]),
    )
    copies = [pltpu.make_async_copy(source, target, sems.at[k]) for k, (source, target) in enumerate(pairs)]
    outs = [pltpu.make_async_copy(cols_ref, cols_out.at[s], out_sems.at[s]) for s in range(Z)]
    outs.append(pltpu.make_async_copy(rows_ref, rows_out, out_sems.at[Z]))
    for copy in copies:
        copy.start()
    for copy in copies[:2]:
        copy.wait()
    for out in outs[:Z]:
        out.start()
    for copy in copies[2:4]:
        copy.wait()
    slots = pairs_ref.shape[1]
    used = lax.broadcasted_iota(jnp.int32, (BLOCKS, slots), 1) < count_ref[0]
    same = lax.broadcasted_iota(jnp.int32, (BLOCKS, slots), 0) == pairs_ref[...]
    hits = jnp.where(same & used, 1.0, 0.0).astype(BF16)
    ones = jnp.ones((MASK_ROWS, slots), BF16)
    flags = lax.dot_general(ones, hits, (((1,), (1,)), ((), ())), preferred_element_type=F32)
    flags = jnp.concatenate([flags, jnp.zeros((MASK_ROWS, WIDTH - BLOCKS), F32)], 1)
    rows_ref[BLOCK:LOAD_ROWS, :] = flags.astype(BF16)
    for copy in copies[4:]:
        copy.wait()
    outs[Z].start()
    for out in outs:
        out.wait()


def tiles(shift, rows_refs, cols_refs, row_acc, first, col_acc):
    owner = lax.axis_index("c") if shift == 0 else 1 - lax.axis_index("c")
    at = lax.axis_index("y") * (Z * C) + owner
    subs = [cols_ref.at[s] for cols_ref in cols_refs for s in range(cols_ref.shape[0])]
    right_probes = jnp.concatenate([sub[:, RANK:WIDTH] for sub in subs], 0)
    rows0, rows1, far_low, far_high, rows3 = rows_refs
    for back, parts in enumerate(((rows0,), (rows1,), (far_low, far_high), (rows3,))):
        loads = [part[...] for part in parts]
        whole = loads[0] if len(loads) == 1 else jnp.concatenate(loads, 0)
        left, left_probes = whole[0:BLOCK, 0:RANK], whole[0:BLOCK, RANK:WIDTH]
        flags = 4.0 * whole[BLOCK:LOAD_ROWS, 0:128].astype(F32)[0:8]
        turned = pltpu.roll(flags, lax.rem(128 - at, 128), 1)
        right = jnp.concatenate(
            [sub[:, 0:RANK] * turned[0:1, C * s : C * s + 1].astype(BF16) for s, sub in enumerate(subs)], 0
        )
        scores = lax.dot_general(
            left, right, (((1,), (1,)), ((), ())), preferred_element_type=F32
        )
        proximity = jnp.log(jnp.maximum(scores, 1.0)).astype(BF16)
        row_part = jnp.dot(proximity, right_probes, preferred_element_type=F32)
        row_acc[back] = row_part if first is None else first[back] + row_part
        col_part = contract_rows(left_probes, proximity)
        if back == 0:
            col_acc[...] = col_part
        else:
            col_acc[...] += col_part
    gram = jnp.dot(jnp.concatenate(split(col_acc[...]), 0), right_probes, preferred_element_type=F32)
    return gram[0:PROBES] + gram[PROBES:]


def own_kernel(rows0, rows1, far_low, far_high, rows3, low_ref, high_ref, row_ref, keep_ref, gram_ref, col_acc):
    gram_ref[...] = tiles(0, (rows0, rows1, far_low, far_high, rows3), (low_ref, high_ref), row_ref, None, col_acc)
    for s in range(Z):
        keep_ref[s] = col_acc[:, s * SUB : (s + 1) * SUB]


def other_kernel(
    rows0, rows1, far_low, far_high, rows3, low_ref, high_ref, first_ref, gram_ref, piece0, piece1, piece2, piece3, send_ref, row_acc, col_acc
):
    gram = tiles(1, (rows0, rows1, far_low, far_high, rows3), (low_ref, high_ref), row_acc, first_ref, col_acc)
    x = lax.axis_index("x")
    for ahead, piece in enumerate((piece0, piece1, piece2, piece3)):
        at = pl.ds(pl.multiple_of(SUB * lax.rem(x + ahead, X), SUB), SUB)
        for back in range(Y):
            piece[back] = row_acc[back, at, :].astype(piece.dtype)
    for s in range(Z):
        send_ref[s] = col_acc[:, s * SUB : (s + 1) * SUB]
    send_ref[Z] = gram_ref[...] + gram


def join_kernel(keep_ref, sent_ref, got_ref, cols_out):
    half = PROBES // C
    at = pl.ds(pl.multiple_of(lax.axis_index("c") * half, half), half)
    parts = split(sent_ref[Z, at, :] + got_ref[Z, at, :])
    for s in range(Z):
        cols_out[s, 0:SUB, :] = (keep_ref[s] + got_ref[s]).astype(BF16)
        for k in range(TERMS):
            cols_out[s, SUB + half * k : SUB + half * (k + 1), :] = parts[k]


def piece_kernel(kept_ref, got1, got2, got3, col_ref, out0, out1, out2, out3, gram_out):
    half = PROBES // C
    gram = col_ref[SUB : SUB + half]
    for k in range(1, TERMS):
        gram += col_ref[SUB + half * k : SUB + half * (k + 1)]
    for k in range(Y * X):
        gram_out[k] = gram
    for back, out in enumerate((out0, out1, out2, out3)):
        total = kept_ref[back]
        for got in (got1, got2, got3):
            total += got[back].astype(F32)
        out[...] = total


def shards(factor_rows, row_side_probes, factor_cols, probe_cols, pair_blocks, pair_count):
    vmem = pl.BlockSpec(memory_space=pltpu.VMEM)
    hbm = pl.BlockSpec(memory_space=pl.ANY)
    params = pltpu.CompilerParams(vmem_limit_bytes=LIMIT)
    shape = jax.ShapeDtypeStruct

    row_load, col_load = pl.pallas_call(
        pack_kernel,
        out_shape=[shape((LOAD_ROWS, WIDTH), BF16), shape((Z, SUB, WIDTH), BF16)],
        in_specs=[hbm] * 6,
        out_specs=[hbm, hbm],
        scratch_shapes=[
            pltpu.SMEM((1,), jnp.int32),
            pltpu.VMEM(pair_blocks.shape, jnp.int32),
            pltpu.VMEM((SUB, WIDTH), BF16),
            pltpu.VMEM((LOAD_ROWS, WIDTH), BF16),
            pltpu.SemaphoreType.DMA((6,)),
            pltpu.SemaphoreType.DMA((Z + 1,)),
        ],
        compiler_params=pltpu.CompilerParams(vmem_limit_bytes=WHOLE),
        name="pack",
    )(pair_count, factor_rows, row_side_probes, factor_cols, probe_cols, pair_blocks)
    near = [lax.ppermute(row_load, "y", ring(Y, s)) for s in (1, 3)]
    far = [lax.ppermute(near[0][:CUT], "y", ring(Y, 1)), lax.ppermute(near[1][CUT:], "y", ring(Y, 3))]
    all_rows = [row_load, near[0], *far, near[1]]
    own_cols = lax.all_to_all(col_load, "z", split_axis=0, concat_axis=0, tiled=True)
    own_cols = [own_cols[: Z // 2], own_cols[Z // 2 :]]
    other_cols = [lax.ppermute(part, "c", SWAP) for part in own_cols]

    cost = pl.CostEstimate(
        flops=2 * Y * BLOCK * HALF * (RANK + 2 * PROBES), bytes_accessed=4 * 2**20, transcendentals=Y * BLOCK * HALF
    )
    first, keep, gram = pl.pallas_call(
        own_kernel,
        out_shape=[shape((Y, BLOCK, PROBES), F32), shape((Z, PROBES, SUB), F32), shape((PROBES, PROBES), F32)],
        in_specs=[vmem] * 7,
        out_specs=[vmem] * 3,
        scratch_shapes=[pltpu.VMEM((PROBES, HALF), F32)],
        compiler_params=params,
        cost_estimate=cost,
        name="own_tiles",
    )(*all_rows, *own_cols)
    *pieces, send = pl.pallas_call(
        other_kernel,
        out_shape=[shape((Y, SUB, PROBES), F32)]
        + [shape((Y, SUB, PROBES), BF16)] * (X - 1)
        + [shape((Z + 1, PROBES, SUB), F32)],
        in_specs=[vmem] * 9,
        out_specs=[vmem] * 5,
        scratch_shapes=[pltpu.VMEM((Y, BLOCK, PROBES), F32), pltpu.VMEM((PROBES, HALF), F32)],
        compiler_params=params,
        cost_estimate=cost,
        name="other_tiles",
    )(*all_rows, *other_cols, first, gram)

    got = lax.ppermute(send, "c", SWAP)
    got_pieces = [lax.ppermute(pieces[s], "x", ring(X, s)) for s in range(1, X)]
    col_load = pl.pallas_call(
        join_kernel,
        out_shape=shape((Z, SENT, SUB), BF16),
        in_specs=[vmem] * 3,
        out_specs=vmem,
        compiler_params=params,
        name="join",
    )(keep, send, got)
    col_got = lax.all_to_all(col_load, "z", split_axis=0, concat_axis=0, tiled=True)
    col_sum = jnp.sum(col_got.astype(F32), 0)
    half = PROBES // C
    col_sketch = col_sum[:SUB].T * SCALE

    *sums, gram = pl.pallas_call(
        piece_kernel,
        out_shape=[shape((SUB, PROBES), F32)] * Y + [shape((Y * X, half, PROBES), F32)],
        in_specs=[vmem] * 5,
        out_specs=[vmem] * 5,
        compiler_params=params,
        name="pieces",
    )(pieces[0], *got_pieces, col_sum)
    got_sums = [lax.ppermute(sums[back], "y", ring(Y, Y - back)) for back in range(1, Y)]
    row_sketch = (sums[0] + got_sums[0] + got_sums[1] + got_sums[2]) * SCALE

    gram = lax.all_to_all(gram, ("y", "x"), split_axis=0, concat_axis=0, tiled=True)
    gram = jnp.sum(gram, 0) * (1.0 / NODES)
    peer = lax.ppermute(gram, "c", SWAP)
    upper = lax.axis_index("c") == 1
    sketch_gram = jnp.concatenate([jnp.where(upper, peer, gram), jnp.where(upper, gram, peer)], 0)
    return (row_sketch, col_sketch, sketch_gram)


def solution(mesh):
    grid = Mesh(mesh.devices.reshape(Y, Z, C, X), ("y", "z", "c", "x"))
    rows, subs = ("y", "z", "c"), ("y", "z", "c", "x")
    return jax.shard_map(
        shards,
        mesh=grid,
        in_specs=(P(rows, None), P(rows, None), P(subs, None), P(subs, None), P(rows, None), P(rows)),
        out_specs=(P(subs, None), P(subs, None), P()),
        check_vma=False,
    )
```

```python
import math

import jax
import jax.numpy as jnp
from jax import lax
from jax.experimental import pallas as pl
from jax.experimental.pallas import tpu as pltpu
from jax.sharding import Mesh, PartitionSpec as P

BF16 = jnp.bfloat16
F32 = jnp.float32
Y, Z, C, X = 4, 8, 2, 4
BLOCKS = Y * Z * C
BLOCK, SUB, RANK, PROBES = 512, 128, 256, 128
WIDTH = RANK + PROBES
MASK_ROWS = 16
LOAD_ROWS = BLOCK + MASK_ROWS
HALF = Z * SUB
CUT = 272
NODES = BLOCKS * BLOCK
TERMS = 1
SENT = SUB + TERMS * PROBES // C
SCALE = 1.0 / math.sqrt(NODES)
LIMIT = 24 * 2**20
WHOLE = 60 * 2**20
SWAP = [(0, 1), (1, 0)]


def ring(size, shift):
    return [(k, (k + shift) % size) for k in range(size)]


def contract_rows(left, right):
    return lax.dot_general(left, right, (((0,), (0,)), ((), ())), preferred_element_type=F32)


def split(value):
    high = value.astype(BF16)
    low = (value - high.astype(F32)).astype(BF16)
    return high, low


def pack_kernel(
    count_hbm, factor_hbm, side_hbm, cols_hbm, probe_hbm, pairs_hbm,
    rows_out, cols_out, count_ref, pairs_ref, cols_ref, rows_ref, sems, out_sems
):
    pairs = (
        (cols_hbm, cols_ref.at[:, 0:RANK]),
        (probe_hbm, cols_ref.at[:, RANK:WIDTH]),
        (count_hbm, count_ref),
        (pairs_hbm, pairs_ref),
        (factor_hbm, rows_ref.at[0:BLOCK, 0:RANK]),
        (side_hbm, rows_ref.at[0:BLOCK, RANK:WIDTH]),
    )
    copies = [pltpu.make_async_copy(source, target, sems.at[k]) for k, (source, target) in enumerate(pairs)]
    outs = [pltpu.make_async_copy(cols_ref, cols_out.at[s], out_sems.at[s]) for s in range(Z)]
    outs.append(pltpu.make_async_copy(rows_ref, rows_out, out_sems.at[Z]))
    for copy in copies:
        copy.start()
    for copy in copies[:2]:
        copy.wait()
    for out in outs[:Z]:
        out.start()
    for copy in copies[2:4]:
        copy.wait()
    slots = pairs_ref.shape[1]
    used = lax.broadcasted_iota(jnp.int32, (BLOCKS, slots), 1) < count_ref[0]
    same = lax.broadcasted_iota(jnp.int32, (BLOCKS, slots), 0) == pairs_ref[...]
    hits = jnp.where(same & used, 1.0, 0.0).astype(BF16)
    ones = jnp.ones((MASK_ROWS, slots), BF16)
    flags = lax.dot_general(ones, hits, (((1,), (1,)), ((), ())), preferred_element_type=F32)
    flags = jnp.concatenate([flags, jnp.zeros((MASK_ROWS, WIDTH - BLOCKS), F32)], 1)
    rows_ref[BLOCK:LOAD_ROWS, :] = flags.astype(BF16)
    for copy in copies[4:]:
        copy.wait()
    outs[Z].start()
    for out in outs:
        out.wait()


def tiles(shift, rows_refs, cols_refs, row_acc, first, col_acc):
    owner = lax.axis_index("c") if shift == 0 else 1 - lax.axis_index("c")
    at = lax.axis_index("y") * (Z * C) + owner
    subs = [cols_ref.at[s] for cols_ref in cols_refs for s in range(cols_ref.shape[0])]
    right_probes = jnp.concatenate([sub[:, RANK:WIDTH] for sub in subs], 0)
    rows0, rows1, far_low, far_high, rows3 = rows_refs
    for back, parts in enumerate(((rows0,), (rows1,), (far_low, far_high), (rows3,))):
        loads = [part[...] for part in parts]
        whole = loads[0] if len(loads) == 1 else jnp.concatenate(loads, 0)
        left, left_probes = whole[0:BLOCK, 0:RANK], whole[0:BLOCK, RANK:WIDTH]
        flags = 4.0 * whole[BLOCK:LOAD_ROWS, 0:128].astype(F32)[0:8]
        turned = pltpu.roll(flags, lax.rem(128 - at, 128), 1)
        right = jnp.concatenate(
            [sub[:, 0:RANK] * turned[0:1, C * s : C * s + 1].astype(BF16) for s, sub in enumerate(subs)], 0
        )
        scores = lax.dot_general(
            left, right, (((1,), (1,)), ((), ())), preferred_element_type=F32
        )
        proximity = jnp.log(jnp.maximum(scores, 1.0)).astype(BF16)
        row_part = jnp.dot(proximity, right_probes, preferred_element_type=F32)
        row_acc[back] = row_part if first is None else first[back] + row_part
        col_part = contract_rows(left_probes, proximity)
        if back == 0:
            col_acc[...] = col_part
        else:
            col_acc[...] += col_part
    gram = jnp.dot(jnp.concatenate(split(col_acc[...]), 0), right_probes, preferred_element_type=F32)
    return gram[0:PROBES] + gram[PROBES:]


def own_kernel(rows0, rows1, far_low, far_high, rows3, low_ref, high_ref, row_ref, keep_ref, gram_ref, col_acc):
    gram_ref[...] = tiles(0, (rows0, rows1, far_low, far_high, rows3), (low_ref, high_ref), row_ref, None, col_acc)
    for s in range(Z):
        keep_ref[s] = col_acc[:, s * SUB : (s + 1) * SUB]


def other_kernel(
    rows0, rows1, far_low, far_high, rows3, low_ref, high_ref, first_ref, gram_ref, piece0, piece1, piece2, piece3, send_ref, row_acc, col_acc
):
    gram = tiles(1, (rows0, rows1, far_low, far_high, rows3), (low_ref, high_ref), row_acc, first_ref, col_acc)
    x = lax.axis_index("x")
    for ahead, piece in enumerate((piece0, piece1, piece2, piece3)):
        at = pl.ds(pl.multiple_of(SUB * lax.rem(x + ahead, X), SUB), SUB)
        for back in range(Y):
            piece[back] = row_acc[back, at, :].astype(piece.dtype)
    for s in range(Z):
        send_ref[s] = col_acc[:, s * SUB : (s + 1) * SUB]
    send_ref[Z] = gram_ref[...] + gram


def join_kernel(keep_ref, sent_ref, got_ref, cols_out):
    half = PROBES // C
    at = pl.ds(pl.multiple_of(lax.axis_index("c") * half, half), half)
    parts = split(sent_ref[Z, at, :] + got_ref[Z, at, :])
    for s in range(Z):
        cols_out[s, 0:SUB, :] = (keep_ref[s] + got_ref[s]).astype(BF16)
        for k in range(TERMS):
            cols_out[s, SUB + half * k : SUB + half * (k + 1), :] = parts[k]


def piece_kernel(kept_ref, got1, got2, got3, col_ref, out0, out1, out2, out3, gram_out):
    half = PROBES // C
    gram = col_ref[SUB : SUB + half]
    for k in range(1, TERMS):
        gram += col_ref[SUB + half * k : SUB + half * (k + 1)]
    for k in range(Y * X):
        gram_out[k] = gram
    for back, out in enumerate((out0, out1, out2, out3)):
        total = kept_ref[back]
        for got in (got1, got2, got3):
            total += got[back].astype(F32)
        out[...] = total


def shards(factor_rows, row_side_probes, factor_cols, probe_cols, pair_blocks, pair_count):
    vmem = pl.BlockSpec(memory_space=pltpu.VMEM)
    hbm = pl.BlockSpec(memory_space=pl.ANY)
    params = pltpu.CompilerParams(vmem_limit_bytes=LIMIT)
    shape = jax.ShapeDtypeStruct

    row_load, col_load = pl.pallas_call(
        pack_kernel,
        out_shape=[shape((LOAD_ROWS, WIDTH), BF16), shape((Z, SUB, WIDTH), BF16)],
        in_specs=[hbm] * 6,
        out_specs=[hbm, hbm],
        scratch_shapes=[
            pltpu.SMEM((1,), jnp.int32),
            pltpu.VMEM(pair_blocks.shape, jnp.int32),
            pltpu.VMEM((SUB, WIDTH), BF16),
            pltpu.VMEM((LOAD_ROWS, WIDTH), BF16),
            pltpu.SemaphoreType.DMA((6,)),
            pltpu.SemaphoreType.DMA((Z + 1,)),
        ],
        compiler_params=pltpu.CompilerParams(vmem_limit_bytes=WHOLE),
        name="pack",
    )(pair_count, factor_rows, row_side_probes, factor_cols, probe_cols, pair_blocks)
    near = [lax.ppermute(row_load, "y", ring(Y, s)) for s in (1, 3)]
    far = [lax.ppermute(near[0][:CUT], "y", ring(Y, 1)), lax.ppermute(near[1][CUT:], "y", ring(Y, 3))]
    all_rows = [row_load, near[0], *far, near[1]]
    own_cols = lax.all_to_all(col_load, "z", split_axis=0, concat_axis=0, tiled=True)
    own_cols = [own_cols[: Z // 2], own_cols[Z // 2 :]]
    other_cols = [lax.ppermute(part, "c", SWAP) for part in own_cols]

    cost = pl.CostEstimate(
        flops=2 * Y * BLOCK * HALF * (RANK + 2 * PROBES), bytes_accessed=4 * 2**20, transcendentals=Y * BLOCK * HALF
    )
    first, keep, gram = pl.pallas_call(
        own_kernel,
        out_shape=[shape((Y, BLOCK, PROBES), F32), shape((Z, PROBES, SUB), F32), shape((PROBES, PROBES), F32)],
        in_specs=[vmem] * 7,
        out_specs=[vmem] * 3,
        scratch_shapes=[pltpu.VMEM((PROBES, HALF), F32)],
        compiler_params=params,
        cost_estimate=cost,
        name="own_tiles",
    )(*all_rows, *own_cols)
    *pieces, send = pl.pallas_call(
        other_kernel,
        out_shape=[shape((Y, SUB, PROBES), F32)]
        + [shape((Y, SUB, PROBES), BF16)] * (X - 1)
        + [shape((Z + 1, PROBES, SUB), F32)],
        in_specs=[vmem] * 9,
        out_specs=[vmem] * 5,
        scratch_shapes=[pltpu.VMEM((Y, BLOCK, PROBES), F32), pltpu.VMEM((PROBES, HALF), F32)],
        compiler_params=params,
        cost_estimate=cost,
        name="other_tiles",
    )(*all_rows, *other_cols, first, gram)

    got = lax.ppermute(send, "c", SWAP)
    got_pieces = [lax.ppermute(pieces[s], "x", ring(X, s)) for s in range(1, X)]
    col_load = pl.pallas_call(
        join_kernel,
        out_shape=shape((Z, SENT, SUB), BF16),
        in_specs=[vmem] * 3,
        out_specs=vmem,
        compiler_params=params,
        name="join",
    )(keep, send, got)
    col_got = lax.all_to_all(col_load, "z", split_axis=0, concat_axis=0, tiled=True)
    col_sum = jnp.sum(col_got.astype(F32), 0)
    half = PROBES // C
    col_sketch = col_sum[:SUB].T * SCALE

    *sums, gram = pl.pallas_call(
        piece_kernel,
        out_shape=[shape((SUB, PROBES), F32)] * Y + [shape((Y * X, half, PROBES), F32)],
        in_specs=[vmem] * 5,
        out_specs=[vmem] * 5,
        compiler_params=params,
        name="pieces",
    )(pieces[0], *got_pieces, col_sum)
    got_sums = [lax.ppermute(sums[back], "y", ring(Y, Y - back)) for back in range(1, Y)]
    row_sketch = (sums[0] + got_sums[0] + got_sums[1] + got_sums[2]) * SCALE

    gram = lax.all_to_all(gram, ("y", "x"), split_axis=0, concat_axis=0, tiled=True)
    gram = jnp.sum(gram, 0) * (1.0 / NODES)
    peer = lax.ppermute(gram, "c", SWAP)
    upper = lax.axis_index("c") == 1
    sketch_gram = jnp.concatenate([jnp.where(upper, peer, gram), jnp.where(upper, gram, peer)], 0)
    return (row_sketch, col_sketch, sketch_gram)


def solution(mesh):
    grid = Mesh(mesh.devices.reshape(Y, Z, C, X), ("y", "z", "c", "x"))
    rows, subs = ("y", "z", "c"), ("y", "z", "c", "x")
    return jax.shard_map(
        shards,
        mesh=grid,
        in_specs=(P(rows, None), P(rows, None), P(subs, None), P(subs, None), P(rows, None), P(rows)),
        out_specs=(P(subs, None), P(subs, None), P()),
        check_vma=False,
    )
```
